512 devices in a mesh: tensor: 4 (over y_hi, core), fsdp: 8 (over z), replica: 16 (over y_lo, x).
Axes of the slice: x: 4, y: 8 (y_hi: 2, y_lo: 4; y = y_hi * 4 + y_lo), z: 8, core: 2. Of those that a mesh axis runs over, the one named last changes fastest.
Arguments:
- activations: bfloat16 [16, 1536, 8192], P('replica', 'fsdp', 'tensor'), may hold values from -6 to 6
- cotangents: bfloat16 [16, 1536, 2, 1024], P('replica', 'fsdp', None, 'tensor'), may hold values from -0.15234375 to 0.15234375
- inner_drift: float32 [16, 8192, 2, 1024], P('replica', ('tensor', 'fsdp')), may hold values from -6 to 6
- drift_flags: int32 [16, 2], P('replica'), may hold values 0 or 1
- master_weights: float32 [8192, 2, 1024], P(('tensor', 'fsdp', 'replica')), may hold values from -3 to 3
- outer_momentum: float32 [8192, 2, 1024], P(('tensor', 'fsdp', 'replica')), may hold values from -3 to 3
Outputs:
- new_master: float32 [8192, 2, 1024], P(('tensor', 'fsdp', 'replica'))
- new_momentum: float32 [8192, 2, 1024], P(('tensor', 'fsdp', 'replica'))
- fresh_copy: bfloat16 [8192, 2, 1024], P(('tensor', 'fsdp'))
The draws below stay inside these ranges and needn't reach their ends.
All inputs are finite; a program needn't handle non-finite values. No bound on the sum of `drift_flags` on one device may be relied on, other than what follows from the above.
Results may differ from the reference program's by a relative error of at most 0.001.
Values may be sent and summed in bfloat16 or wider, within the bound.
No kernel may reach another device: no remote copies, remote signals or barrier semaphores. Data moves between devices by JAX's collectives and lax.ppermute only.
A program may use at most 64 MiB of HBM per device.

```python
import jax
import jax.numpy as jnp
from jax import lax

D = 8192
KVW = 1024
TOKENS = 1536
REPLICAS = 16


def set_ends(array, own_key, least, top_value):
    place = [jax.random.randint(jax.random.fold_in(own_key, axis), (), 0, length) for axis, length in enumerate(array.shape)]
    main_axis = array.shape.index(max(array.shape))
    next_to = place[:main_axis] + [(place[main_axis] + 1) % array.shape[main_axis]] + place[main_axis + 1:]
    return array.at[tuple(place)].set(least).at[tuple(next_to)].set(top_value)


def raised(values, own_key, source, target, blocks, factor):
    owner, partner = [(jnp.arange(values.shape[dim]) // (values.shape[dim] // blocks)).reshape([-1 if axis == dim else 1 for axis in range(values.ndim)]) for dim in (source, target)]
    chosen = jax.random.permutation(own_key, blocks)[partner]
    strong = (owner == chosen) | (owner == (partner + blocks // 2) % blocks)
    return jnp.where(strong, factor * values, values)


def levels(stream_key, shape, pieces, smallest, largest):
    def one(position, shards_of):
        steps = jax.random.uniform(jax.random.fold_in(jax.random.fold_in(stream_key, 6), position), (shards_of,), jnp.float32, smallest / len(pieces), largest / len(pieces))
        return jnp.repeat(jnp.exp(steps), shape[position] // shards_of).reshape((-1,) + (1,) * (len(shape) - position - 1))

    level = one(*pieces[0])
    for cut in pieces[1:]:
        level = level * one(*cut)
    return level


def normal_values(stream_key, shape, deviation, most, cuts=(), held_as=jnp.bfloat16):
    array = jax.random.normal(stream_key, shape, jnp.float32) * deviation
    if len(cuts) > 0:
        array = levels(stream_key, shape, cuts, -0.22, 0.18) * array
    return jnp.clip(array, min=-most, max=most).astype(held_as)


def noise_with(stream_key, extent, scale, reach, cuts, heavy, kind=jnp.bfloat16):
    result = scale * jax.random.normal(stream_key, extent, jnp.float32)
    if cuts:
        result = result * levels(stream_key, extent, cuts, -0.22, 0.18)
    return jnp.clip(raised(result, jax.random.fold_in(stream_key, 3), *heavy), -reach, reach).astype(kind)


def setup_inputs(seed: int = 0) -> dict:
    key_list = jax.random.split(jax.random.key(seed), 7)
    return {
        "activations": normal_values(key_list[0], (REPLICAS, TOKENS, D), 1.0, 6.0, ((0, 16), (1, 8), (2, 4))),
        "cotangents": normal_values(key_list[1], (REPLICAS, TOKENS, 2, KVW), (1.0 / TOKENS ** 0.5), 0.15234375, ((0, 16), (1, 8), (3, 4))),
        "inner_drift": noise_with(key_list[2], (REPLICAS, D, 2, KVW), 1.0, 6.0, ((0, 16), (1, 32)), (0, 1, 16, 2.0), jnp.float32),
        "drift_flags": set_ends((jax.random.randint(key_list[3], (REPLICAS, 2), 0, 4) < 3).astype(jnp.int32), jax.random.fold_in(key_list[3], 1), 0, 1),
        "master_weights": normal_values(key_list[4], (D, 2, KVW), 0.5, 3.0, ((0, 512),), jnp.float32),
        "outer_momentum": normal_values(key_list[5], (D, 2, KVW), 0.5, 3.0, ((0, 512),), jnp.float32),
    }


inner_rate = 0.8
momentum_decay = 0.9
outer_rate = 0.7


def reference(activations, cotangents, inner_drift, drift_flags, master_weights, outer_momentum):
    def one_worker(summed, items):
        worker_acts, worker_cots, worker_drift, worker_flags = items
        gradient = lax.dot_general(worker_acts, worker_cots.reshape(TOKENS, 2 * KVW), (((0,), (0,)), ((), ())), preferred_element_type=jnp.float32)
        gradient = gradient.reshape(D, 2, KVW)
        weighting = worker_flags.astype(jnp.float32)[None, :, None]
        return summed + weighting * (worker_drift + inner_rate * gradient), None

    start_sum = jnp.zeros((D, 2, KVW), jnp.float32)
    drift_sum, unused = lax.scan(one_worker, start_sum, (activations, cotangents, inner_drift, drift_flags))
    delta = drift_sum / REPLICAS
    new_momentum = momentum_decay * outer_momentum + delta
    new_master = master_weights - outer_rate * (delta + momentum_decay * new_momentum)
    return new_master, new_momentum, new_master.astype(jnp.bfloat16)
```

```python
import jax
import jax.numpy as jnp
from jax import lax
from jax.sharding import Mesh, PartitionSpec as P

inner_rate = 0.8
momentum_decay = 0.9
outer_rate = 0.7

f32, f16, bf16 = jnp.float32, jnp.float16, jnp.bfloat16


def body(activations, cotangents, inner_drift, drift_flags, master_weights, outer_momentum):
    n_yh, n_core, n_z, n_yl, n_x = (lax.axis_size(a) for a in ("yh", "core", "z", "yl", "x"))
    replicas = n_yl * n_x
    core = lax.axis_index("core")
    tokens, width = activations.shape[1], activations.shape[2]
    heads = cotangents.shape[3]
    own_rows = master_weights.shape[0]
    rows, kvw = inner_drift.shape[1], inner_drift.shape[3]

    by_k = cotangents[0].swapaxes(0, 1)[None]
    by_k = jnp.broadcast_to(by_k, (n_yh, 2, tokens, heads)).reshape(n_yh * 2, tokens, heads)
    parts = lax.all_to_all(by_k, ("yh", "core"), 0, 0, tiled=True)
    mine = parts.swapaxes(0, 1).reshape(tokens, kvw)
    mine, acts, drift = lax.optimization_barrier((mine, activations[0], inner_drift[0]))
    portion = lax.all_gather(mine, "z", axis=0, tiled=True)

    acts = acts.reshape(tokens, n_z, rows).swapaxes(0, 1)
    acts = lax.all_to_all(acts, "z", 0, 0, tiled=True).reshape(n_z * tokens, rows)
    acts_pair = lax.all_to_all(jnp.broadcast_to(acts[None], (n_core,) + acts.shape), "core", 0, 0, tiled=True)

    drift_pair = lax.all_to_all(drift.swapaxes(0, 1), "core", 0, 0, tiled=True)

    flag = lax.dynamic_index_in_dim(drift_flags[0], core, 0, keepdims=False).astype(f32)
    grads = lax.dot_general(acts_pair, portion, (((1,), (0,)), ((), ())), preferred_element_type=f32)
    term = flag * (drift_pair + inner_rate * grads)

    sent = term.astype(f16).reshape(n_core, n_yl, n_x, own_rows, kvw).transpose(2, 0, 1, 3, 4)
    got = lax.all_to_all(sent, "x", 0, 0, tiled=True)
    half = got.astype(f32).sum(0).astype(f16).reshape(n_core * n_yl, own_rows, kvw)
    got = lax.all_to_all(half, ("core", "yl"), 0, 0, tiled=True)
    drift_sum = got.astype(f32).reshape(2, n_yl, own_rows, kvw).sum(1).swapaxes(0, 1)

    delta = drift_sum / replicas
    new_momentum = momentum_decay * outer_momentum + delta
    new_master = master_weights - outer_rate * (delta + momentum_decay * new_momentum)

    fresh = new_master.astype(bf16)
    fresh = jnp.broadcast_to(fresh[None], (n_yl, own_rows, 2, kvw))
    fresh = lax.all_to_all(fresh, "yl", 0, 0, tiled=True)
    fresh = jnp.broadcast_to(fresh[None], (n_x, n_yl, own_rows, 2, kvw))
    fresh = lax.all_to_all(fresh, "x", 0, 0, tiled=True)
    fresh_copy = fresh.swapaxes(0, 1).reshape(rows, 2, kvw)
    return (new_master, new_momentum, fresh_copy)


def solution(mesh):
    split = Mesh(mesh.devices.reshape(2, 2, 8, 4, 4), ("yh", "core", "z", "yl", "x"))
    tensor, replica = ("yh", "core"), ("yl", "x")
    return jax.shard_map(
        body,
        mesh=split,
        in_specs=(
            P(replica, "z", tensor),
            P(replica, "z", None, tensor),
            P(replica, tensor + ("z",), None, None),
            P(replica, None),
            P(tensor + ("z",) + replica, None, None),
            P(tensor + ("z",) + replica, None, None),
        ),
        out_specs=(
            P(tensor + ("z",) + replica, None, None),
            P(tensor + ("z",) + replica, None, None),
            P(tensor + ("z",), None, None),
        ),
        check_vma=False,
    )
```

```python
import jax
import jax.numpy as jnp
from jax import lax
from jax.sharding import Mesh, PartitionSpec as P

inner_rate = 0.8
momentum_decay = 0.9
outer_rate = 0.7

f32, f16, bf16 = jnp.float32, jnp.float16, jnp.bfloat16


def body(activations, cotangents, inner_drift, drift_flags, master_weights, outer_momentum):
    n_z, replicas = lax.axis_size("z"), lax.axis_size("yl") * lax.axis_size("x")
    first_core = lax.axis_index("core") == 0
    low_half = lax.axis_index("yh") == 0
    z = lax.axis_index("z")
    tokens = activations.shape[1]
    part = tokens // 2
    own_rows = master_weights.shape[0]
    rows, kvw = inner_drift.shape[1], inner_drift.shape[3]
    half = kvw // 2

    def swap(value, axis):
        return lax.ppermute(value, axis, [(0, 1), (1, 0)])

    ways = [(i, (i + 1) % n_z) for i in range(n_z)] + [(n_z + i, n_z + (i - 1) % n_z) for i in range(n_z)]

    def step(value):
        return lax.ppermute(value, ("core", "z"), ways)

    def cut(block, first):
        return jnp.where(first, block[:part], block[part:])

    def chip(mine, other):
        low, high = jnp.where(first_core, mine, other), jnp.where(first_core, other, mine)
        return jnp.concatenate([low[0], high[0], low[1], high[1]], axis=1)

    def ring(block):
        held = [cut(block, first_core)]
        for _ in range(n_z // 2 - 1):
            block = step(block)
            held.append(block)
        held.append(step(cut(block, first_core)))
        return jnp.concatenate(held, axis=0)

    cots = cotangents[0].swapaxes(0, 1)
    far = swap(cots, "yh")
    near_columns = ring(chip(cots, swap(cots, "core")))
    far_columns = ring(chip(far, swap(far, "core")))

    acts = activations[0].reshape(tokens, n_z, rows).swapaxes(0, 1)
    acts = lax.all_to_all(acts, "z", 0, 0, tiled=True)

    def in_order(first):
        sign = jnp.where(first, -1, 1)
        blocks = [lax.dynamic_index_in_dim(acts, (z + n_z + sign * s) % n_z, 0, keepdims=False) for s in range(n_z // 2 + 1)]
        return jnp.concatenate([cut(blocks[0], first)] + blocks[1:-1] + [cut(blocks[-1], first)], axis=0)

    acts_mine = in_order(first_core)
    acts_other = swap(in_order(~first_core), "core")

    def gradient(columns):
        dims = (((0,), (0,)), ((), ()))
        theirs = lax.dot_general(acts_other, columns, dims, preferred_element_type=f32)
        came = swap(theirs, "core")
        return lax.dot_general(acts_mine, columns, dims, preferred_element_type=f32) + came

    drift = inner_drift[0].swapaxes(0, 1)
    flags = drift_flags[0].astype(f32)

    def terms(columns, low):
        grads = gradient(columns)
        drifts = jnp.where(low, drift[:, :, :half], drift[:, :, half:])
        return jnp.concatenate(
            [flags[k] * (drifts[k] + inner_rate * grads[:, k * half : (k + 1) * half]) for k in range(2)], axis=1
        ).astype(f16)

    def reduced(term):
        got = lax.all_to_all(term.reshape(replicas, own_rows, -1), ("yl", "x"), 0, 0, tiled=True)
        return got.astype(f32).sum(0)

    total = reduced(jnp.concatenate([terms(near_columns, low_half), terms(far_columns, ~low_half)], axis=1))
    total = total.reshape(own_rows, 2, 2, half)
    low, high = jnp.where(low_half, total[:, 0], total[:, 1]), jnp.where(low_half, total[:, 1], total[:, 0])
    drift_sum = jnp.concatenate([low, high], axis=2)

    delta = drift_sum / replicas
    new_momentum = momentum_decay * outer_momentum + delta
    new_master = master_weights - outer_rate * (delta + momentum_decay * new_momentum)

    fresh = jnp.broadcast_to(new_master.astype(bf16)[None], (replicas, own_rows, 2, kvw))
    fresh_copy = lax.all_to_all(fresh, ("yl", "x"), 0, 0, tiled=True).reshape(rows, 2, kvw)
    return (new_master, new_momentum, fresh_copy)


def solution(mesh):
    split = Mesh(mesh.devices.reshape(2, 2, 8, 4, 4), ("yh", "core", "z", "yl", "x"))
    tensor, replica = ("yh", "core"), ("yl", "x")
    return jax.shard_map(
        body,
        mesh=split,
        in_specs=(
            P(replica, "z", tensor),
            P(replica, "z", None, tensor),
            P(replica, tensor + ("z",), None, None),
            P(replica, None),
            P(tensor + ("z",) + replica, None, None),
            P(tensor + ("z",) + replica, None, None),
        ),
        out_specs=(
            P(tensor + ("z",) + replica, None, None),
            P(tensor + ("z",) + replica, None, None),
            P(tensor + ("z",), None, None),
        ),
        check_vma=False,
    )
```

```python
import jax
import jax.numpy as jnp
from jax import lax
from jax.sharding import Mesh, PartitionSpec as P

inner_rate = 0.8
momentum_decay = 0.9
outer_rate = 0.7

f32, f16, bf16 = jnp.float32, jnp.float16, jnp.bfloat16


def body(activations, cotangents, inner_drift, drift_flags, master_weights, outer_momentum):
    n_z, replicas = lax.axis_size("z"), lax.axis_size("yl") * lax.axis_size("x")
    first_core = lax.axis_index("core") == 0
    low_half = lax.axis_index("yh") == 0
    z = lax.axis_index("z")
    tokens = activations.shape[1]
    part = tokens // 2
    own_rows = master_weights.shape[0]
    rows, kvw = inner_drift.shape[1], inner_drift.shape[3]
    half = kvw // 2

    def swap(value, axis):
        return lax.ppermute(value, axis, [(0, 1), (1, 0)])

    ways = [(i, (i + 1) % n_z) for i in range(n_z)] + [(n_z + i, n_z + (i - 1) % n_z) for i in range(n_z)]

    def step(value):
        return lax.ppermute(value, ("core", "z"), ways)

    def tied(*values):
        return lax.optimization_barrier(values)

    def cut(block, first):
        return jnp.where(first, block[:part], block[part:])

    def chip(mine, other):
        low, high = jnp.where(first_core, mine, other), jnp.where(first_core, other, mine)
        return jnp.concatenate([low[0], high[0], low[1], high[1]], axis=1)

    cots = cotangents[0].swapaxes(0, 1)
    near = chip(cots, swap(cots, "core"))
    near, cots, own_acts, drift = lax.optimization_barrier((near, cots, activations[0], inner_drift[0]))
    far = swap(cots, "yh")

    near_held = [cut(near, first_core)]
    for _ in range(2):
        near = step(near)
        near_held.append(near)
    far = chip(far, swap(far, "core"))
    near, far = tied(near, far)
    far_held = [cut(far, first_core)]
    near, far = step(near), step(far)
    near_held.append(near)
    far_held.append(far)
    near, far = tied(near, far)
    near, far = step(cut(near, first_core)), step(far)
    near_held.append(near)
    far_held.append(far)
    near, far = tied(near, far)
    far = step(far)
    far_held.append(far)

    acts = own_acts.reshape(tokens, n_z, rows).swapaxes(0, 1)
    acts = lax.all_to_all(acts, "z", 0, 0, tiled=True)

    def in_order(first):
        sign = jnp.where(first, -1, 1)
        blocks = [lax.dynamic_index_in_dim(acts, (z + n_z + sign * s) % n_z, 0, keepdims=False) for s in range(n_z // 2 + 1)]
        return jnp.concatenate([cut(blocks[0], first)] + blocks[1:-1] + [cut(blocks[-1], first)], axis=0)

    acts_mine = in_order(first_core)
    acts_other = swap(in_order(~first_core), "core")

    drift = drift.swapaxes(0, 1)
    flags = drift_flags[0].astype(f32)
    by_column = jnp.repeat(flags, half)[None]

    def own_term(held, low, before=None):
        columns = jnp.concatenate(held, axis=0)
        drifts = jnp.where(low, drift[:, :, :half], drift[:, :, half:])
        drifts = jnp.concatenate([drifts[0], drifts[1]], axis=1)
        dims = (((0,), (0,)), ((), ()))
        theirs = lax.dot_general(acts_other, columns, dims, preferred_element_type=f32)
        came = swap(theirs, "core")
        if before is not None:
            before, came = tied(before, came)
        grads = lax.dot_general(acts_mine, columns, dims, preferred_element_type=f32) + came
        return (by_column * (drifts + inner_rate * grads)).astype(f16), before

    def summed(term):
        got = lax.all_to_all(term.reshape(replicas, own_rows, 2 * half), ("yl", "x"), 0, 0, tiled=True)
        return got.astype(f32).sum(0).reshape(own_rows, 2, half)

    near_term, far = tied(own_term(near_held, low_half)[0], cut(far, first_core))
    near_sum = summed(near_term)
    far_held.append(step(far))
    far_term, near_sum = own_term(far_held, ~low_half, near_sum)
    far_sum = summed(far_term)
    low, high = jnp.where(low_half, near_sum, far_sum), jnp.where(low_half, far_sum, near_sum)
    drift_sum = jnp.concatenate([low, high], axis=2)

    delta = drift_sum / replicas
    new_momentum = momentum_decay * outer_momentum + delta
    new_master = master_weights - outer_rate * (delta + momentum_decay * new_momentum)

    fresh = jnp.broadcast_to(new_master.astype(bf16)[None], (replicas, own_rows, 2, kvw))
    fresh_copy = lax.all_to_all(fresh, ("yl", "x"), 0, 0, tiled=True).reshape(rows, 2, kvw)
    return (new_master, new_momentum, fresh_copy)


def solution(mesh):
    split = Mesh(mesh.devices.reshape(2, 2, 8, 4, 4), ("yh", "core", "z", "yl", "x"))
    tensor, replica = ("yh", "core"), ("yl", "x")
    return jax.shard_map(
        body,
        mesh=split,
        in_specs=(
            P(replica, "z", tensor),
            P(replica, "z", None, tensor),
            P(replica, tensor + ("z",), None, None),
            P(replica, None),
            P(tensor + ("z",) + replica, None, None),
            P(tensor + ("z",) + replica, None, None),
        ),
        out_specs=(
            P(tensor + ("z",) + replica, None, None),
            P(tensor + ("z",) + replica, None, None),
            P(tensor + ("z",), None, None),
        ),
        check_vma=False,
    )
```

```python
import jax
import jax.numpy as jnp
from jax import lax
from jax.sharding import Mesh, PartitionSpec as P

inner_rate = 0.8
momentum_decay = 0.9
outer_rate = 0.7

f32, f16, bf16 = jnp.float32, jnp.float16, jnp.bfloat16


def body(activations, cotangents, inner_drift, drift_flags, master_weights, outer_momentum):
    n_core, n_z, n_yl, n_x = (lax.axis_size(a) for a in ("core", "z", "yl", "x"))
    replicas = n_yl * n_x
    core = lax.axis_index("core")
    tokens, width = activations.shape[1], activations.shape[2]
    own_rows = master_weights.shape[0]
    rows, kvw = inner_drift.shape[1], inner_drift.shape[3]

    low_half = lax.axis_index("yh") == 0
    first_core = core == 0

    def swap(value, axis):
        return lax.ppermute(value, axis, [(0, 1), (1, 0)])

    def ordered(first, mine, other):
        return [jnp.where(first, mine, other), jnp.where(first, other, mine)]

    def of_core(pair):
        kept, sent = ordered(first_core, pair[0], pair[1])
        return jnp.concatenate(ordered(first_core, kept, swap(sent, "core")), axis=1)

    acts = activations[0].reshape(tokens, n_z, rows).swapaxes(0, 1)
    acts = lax.all_to_all(acts, "z", 0, 0, tiled=True).reshape(n_z * tokens, rows)
    cots = cotangents[0].swapaxes(0, 1)
    mine = jnp.concatenate(ordered(low_half, of_core(cots), of_core(swap(cots, "yh"))), axis=1)

    mine, acts, drift = lax.optimization_barrier((mine, acts, inner_drift[0]))
    portion = lax.all_gather(mine, "z", axis=0, tiled=True)

    acts_pair = lax.all_to_all(jnp.broadcast_to(acts[None], (n_core,) + acts.shape), "core", 0, 0, tiled=True)

    drift_pair = lax.all_to_all(drift.swapaxes(0, 1), "core", 0, 0, tiled=True)

    flag = lax.dynamic_index_in_dim(drift_flags[0], core, 0, keepdims=False).astype(f32)
    grads = lax.dot_general(acts_pair, portion, (((1,), (0,)), ((), ())), preferred_element_type=f32)
    term = flag * (drift_pair + inner_rate * grads)

    sent = term.astype(f16).reshape(n_core * replicas, own_rows, kvw)
    got = lax.all_to_all(sent, ("core", "yl", "x"), 0, 0, tiled=True)
    drift_sum = got.astype(f32).reshape(2, replicas, own_rows, kvw).sum(1).swapaxes(0, 1)

    delta = drift_sum / replicas
    new_momentum = momentum_decay * outer_momentum + delta
    new_master = master_weights - outer_rate * (delta + momentum_decay * new_momentum)

    fresh = jnp.broadcast_to(new_master.astype(bf16)[None], (replicas, own_rows, 2, kvw))
    fresh_copy = lax.all_to_all(fresh, ("yl", "x"), 0, 0, tiled=True).reshape(rows, 2, kvw)
    return (new_master, new_momentum, fresh_copy)


def solution(mesh):
    split = Mesh(mesh.devices.reshape(2, 2, 8, 4, 4), ("yh", "core", "z", "yl", "x"))
    tensor, replica = ("yh", "core"), ("yl", "x")
    return jax.shard_map(
        body,
        mesh=split,
        in_specs=(
            P(replica, "z", tensor),
            P(replica, "z", None, tensor),
            P(replica, tensor + ("z",), None, None),
            P(replica, None),
            P(tensor + ("z",) + replica, None, None),
            P(tensor + ("z",) + replica, None, None),
        ),
        out_specs=(
            P(tensor + ("z",) + replica, None, None),
            P(tensor + ("z",) + replica, None, None),
            P(tensor + ("z",), None, None),
        ),
        check_vma=False,
    )
```

```python
import functools

import jax
import jax.numpy as jnp
from jax import lax
from jax.experimental import pallas as pl
from jax.experimental.pallas import tpu as pltpu
from jax.sharding import Mesh, PartitionSpec as P

inner_rate = 0.8
momentum_decay = 0.9
outer_rate = 0.7

f32, f16, bf16 = jnp.float32, jnp.float16, jnp.bfloat16


def product_kernel(n, place, acts, *rest):
    blocks, out = rest[:n], rest[n]
    part = blocks[0].shape[0] // 2
    first, second = (pl.ds(pl.multiple_of(place[n + i], 32), part) for i in range(2))
    for i, block in enumerate(blocks):
        tokens = acts[place[i], first, :]
        if 0 < i < n - 1:
            tokens = jnp.concatenate([tokens, acts[place[i], second, :]], axis=0)
        value = block[...] if i > 0 else block[:part]
        product = lax.dot_general(tokens, value, (((0,), (0,)), ((), ())), preferred_element_type=f32)
        if i == 0:
            out[...] = product
        else:
            out[...] += product


def product(place, acts, blocks):
    rows, columns = acts.shape[2], blocks[0].shape[1]
    depth = acts.shape[0] * acts.shape[1] // 2
    return pl.pallas_call(
        functools.partial(product_kernel, len(blocks)),
        out_shape=jax.ShapeDtypeStruct((rows, columns), f32),
        in_specs=[pl.BlockSpec(memory_space=pltpu.SMEM)] + [pl.BlockSpec(memory_space=pltpu.VMEM)] * (1 + len(blocks)),
        out_specs=pl.BlockSpec(memory_space=pltpu.VMEM),
        compiler_params=pltpu.CompilerParams(vmem_limit_bytes=24 * 2**20),
        cost_estimate=pl.CostEstimate(
            flops=2 * depth * rows * columns, bytes_accessed=2 * depth * (rows + columns) + 4 * rows * columns, transcendentals=0
        ),
        name="token_half_product",
    )(place, acts, *blocks)


def body(activations, cotangents, inner_drift, drift_flags, master_weights, outer_momentum):
    n_z, replicas = lax.axis_size("z"), lax.axis_size("yl") * lax.axis_size("x")
    first_core = lax.axis_index("core") == 0
    low_half = lax.axis_index("yh") == 0
    z = lax.axis_index("z")
    tokens = activations.shape[1]
    part = tokens // 2
    own_rows = master_weights.shape[0]
    rows, kvw = inner_drift.shape[1], inner_drift.shape[3]
    half = kvw // 2

    def swap(value, axis):
        return lax.ppermute(value, axis, [(0, 1), (1, 0)])

    ways = [(i, (i + 1) % n_z) for i in range(n_z)] + [(n_z + i, n_z + (i - 1) % n_z) for i in range(n_z)]

    def step(value):
        return lax.ppermute(value, ("core", "z"), ways)

    def tied(*values):
        return lax.optimization_barrier(values)

    def chip(mine, other):
        mine, other = ([jnp.where(first_core, v, jnp.roll(v, part, axis=0)) for v in (w[0], w[1])] for w in (mine, other))
        pairs = [jnp.where(first_core, a, b) for k in range(2) for a, b in ((mine[k], other[k]), (other[k], mine[k]))]
        return jnp.concatenate(pairs, axis=1)

    def ring(block):
        held = [block]
        for _ in range(n_z // 2 - 1):
            block = step(block)
            held.append(block)
        held.append(step(block[:part]))
        return held

    acts = activations[0].reshape(tokens, n_z, rows).swapaxes(0, 1)
    acts = lax.all_to_all(acts, "z", 0, 0, tiled=True)
    acts_other = swap(acts, "core")
    sign = jnp.where(first_core, -1, 1)
    places = [(z + n_z + sign * s) % n_z for s in range(n_z // 2 + 1)]
    place = jnp.stack(places + [jnp.where(first_core, 0, part), jnp.where(first_core, part, 0)]).astype(jnp.int32)

    cots = cotangents[0].swapaxes(0, 1)
    far = swap(cots, "yh")
    near_held = ring(chip(cots, swap(cots, "core")))
    far_held = ring(chip(far, swap(far, "core")))

    flags = jnp.repeat(drift_flags[0].astype(f32), half)[None]
    drift = inner_drift[0].swapaxes(0, 1)

    def half_of(low):
        return jnp.concatenate(list(jnp.where(low, drift[:, :, :half], drift[:, :, half:])), axis=1)

    near_drift, far_drift, acts_other = tied(half_of(low_half), half_of(~low_half), acts_other)

    def term(held, drifts):
        came = swap(product(place, acts_other, held), "core")
        grads = product(place, acts, held) + came
        return (flags * (drifts + inner_rate * grads)).astype(f16)

    def reduced(value):
        got = lax.all_to_all(value.reshape(replicas, own_rows, -1), ("yl", "x"), 0, 0, tiled=True)
        return got.astype(f32).sum(0)

    near_term = term(near_held, near_drift)
    total = reduced(jnp.concatenate([near_term, term(far_held, far_drift)], axis=1))
    total = total.reshape(own_rows, 2, 2, half)
    low, high = jnp.where(low_half, total[:, 0], total[:, 1]), jnp.where(low_half, total[:, 1], total[:, 0])
    drift_sum = jnp.concatenate([low, high], axis=2)

    delta = drift_sum / replicas
    new_momentum = momentum_decay * outer_momentum + delta
    new_master = master_weights - outer_rate * (delta + momentum_decay * new_momentum)

    fresh = jnp.broadcast_to(new_master.astype(bf16)[None], (replicas, own_rows, 2, kvw))
    fresh_copy = lax.all_to_all(fresh, ("yl", "x"), 0, 0, tiled=True).reshape(rows, 2, kvw)
    return (new_master, new_momentum, fresh_copy)


def solution(mesh):
    split = Mesh(mesh.devices.reshape(2, 2, 8, 4, 4), ("yh", "core", "z", "yl", "x"))
    tensor, replica = ("yh", "core"), ("yl", "x")
    return jax.shard_map(
        body,
        mesh=split,
        in_specs=(
            P(replica, "z", tensor),
            P(replica, "z", None, tensor),
            P(replica, tensor + ("z",), None, None),
            P(replica, None),
            P(tensor + ("z",) + replica, None, None),
            P(tensor + ("z",) + replica, None, None),
        ),
        out_specs=(
            P(tensor + ("z",) + replica, None, None),
            P(tensor + ("z",) + replica, None, None),
            P(tensor + ("z",), None, None),
        ),
        check_vma=False,
    )
```

```python
import functools

import jax
import jax.numpy as jnp
from jax import lax
from jax.experimental import pallas as pl
from jax.experimental.pallas import tpu as pltpu
from jax.sharding import Mesh, PartitionSpec as P

inner_rate = 0.8
momentum_decay = 0.9
outer_rate = 0.7

f32, f16, bf16 = jnp.float32, jnp.float16, jnp.bfloat16


def product_kernel(n, place, acts, *rest):
    blocks, out = rest[:n], rest[n]
    part = blocks[0].shape[0] // 2
    first, second = (pl.ds(pl.multiple_of(place[n + i], 32), part) for i in range(2))
    for i, block in enumerate(blocks):
        tokens = acts[place[i], first, :]
        if 0 < i < n - 1:
            tokens = jnp.concatenate([tokens, acts[place[i], second, :]], axis=0)
        value = block[...] if i > 0 else block[:part]
        product = lax.dot_general(tokens, value, (((0,), (0,)), ((), ())), preferred_element_type=f32)
        if i == 0:
            out[...] = product
        else:
            out[...] += product


def product(place, acts, blocks):
    rows, columns = acts.shape[2], blocks[0].shape[1]
    depth = acts.shape[0] * acts.shape[1] // 2
    return pl.pallas_call(
        functools.partial(product_kernel, len(blocks)),
        out_shape=jax.ShapeDtypeStruct((rows, columns), f32),
        in_specs=[pl.BlockSpec(memory_space=pltpu.SMEM)] + [pl.BlockSpec(memory_space=pltpu.VMEM)] * (1 + len(blocks)),
        out_specs=pl.BlockSpec(memory_space=pltpu.VMEM),
        compiler_params=pltpu.CompilerParams(vmem_limit_bytes=24 * 2**20),
        cost_estimate=pl.CostEstimate(
            flops=2 * depth * rows * columns, bytes_accessed=2 * depth * (rows + columns) + 4 * rows * columns, transcendentals=0
        ),
        name="token_half_product",
    )(place, acts, *blocks)


def body(activations, cotangents, inner_drift, drift_flags, master_weights, outer_momentum):
    n_z, replicas = lax.axis_size("z"), lax.axis_size("yl") * lax.axis_size("x")
    first_core = lax.axis_index("core") == 0
    low_half = lax.axis_index("yh") == 0
    z = lax.axis_index("z")
    tokens = activations.shape[1]
    part = tokens // 2
    own_rows = master_weights.shape[0]
    rows, kvw = inner_drift.shape[1], inner_drift.shape[3]
    half = kvw // 2

    def swap(value, axis):
        return lax.ppermute(value, axis, [(0, 1), (1, 0)])

    ways = [(i, (i + 1) % n_z) for i in range(n_z)] + [(n_z + i, n_z + (i - 1) % n_z) for i in range(n_z)]

    def step(value):
        return lax.ppermute(value, ("core", "z"), ways)

    def tied(*values):
        return lax.optimization_barrier(values)

    def chip(mine, other):
        mine, other = ([jnp.where(first_core, v, jnp.roll(v, part, axis=0)) for v in (w[0], w[1])] for w in (mine, other))
        pairs = [jnp.where(first_core, a, b) for k in range(2) for a, b in ((mine[k], other[k]), (other[k], mine[k]))]
        return jnp.concatenate(pairs, axis=1)

    def ring(first, block):
        held = [first, block]
        for _ in range(n_z // 2 - 2):
            block = step(block)
            held.append(block)
        held.append(step(block[:part]))
        return held

    acts = activations[0].reshape(tokens, n_z, rows).swapaxes(0, 1)
    acts = lax.all_to_all(acts, "z", 0, 0, tiled=True)
    acts_other = swap(acts, "core")
    sign = jnp.where(first_core, -1, 1)
    places = [(z + n_z + sign * s) % n_z for s in range(n_z // 2 + 1)]
    place = jnp.stack(places + [jnp.where(first_core, 0, part), jnp.where(first_core, part, 0)]).astype(jnp.int32)

    flags = jnp.repeat(drift_flags[0].astype(f32), half)[None]
    cots = cotangents[0].swapaxes(0, 1)
    far = swap(cots, "yh")
    near = chip(cots, swap(cots, "core"))
    far = chip(far, swap(far, "core"))

    far, drift = tied(far, inner_drift[0])
    drift = drift.swapaxes(0, 1)

    def half_of(low):
        return jnp.concatenate(list(jnp.where(low, drift[:, :, :half], drift[:, :, half:])), axis=1)

    near_next, far_next, near_drift, far_drift = tied(step(near), step(far), half_of(low_half), half_of(~low_half))
    near_held, far_held = ring(near, near_next), ring(far, far_next)

    def term(held, drifts):
        came = swap(product(place, acts_other, held), "core")
        grads = product(place, acts, held) + came
        return (flags * (drifts + inner_rate * grads)).astype(f16)

    def reduced(value):
        got = lax.all_to_all(value.reshape(replicas, own_rows, -1), ("yl", "x"), 0, 0, tiled=True)
        return got.astype(f32).sum(0)

    near_term = term(near_held, near_drift)
    total = reduced(jnp.concatenate([near_term, term(far_held, far_drift)], axis=1))
    total = total.reshape(own_rows, 2, 2, half)
    low, high = jnp.where(low_half, total[:, 0], total[:, 1]), jnp.where(low_half, total[:, 1], total[:, 0])
    drift_sum = jnp.concatenate([low, high], axis=2)

    delta = drift_sum / replicas
    new_momentum = momentum_decay * outer_momentum + delta
    new_master = master_weights - outer_rate * (delta + momentum_decay * new_momentum)

    n_yl, n_x = lax.axis_size("yl"), lax.axis_size("x")
    fresh = jnp.broadcast_to(new_master.astype(bf16)[None], (n_yl, own_rows, 2, kvw))
    fresh = lax.all_to_all(fresh, "yl", 0, 0, tiled=True)
    fresh = jnp.broadcast_to(fresh[None], (n_x, n_yl, own_rows, 2, kvw))
    fresh = lax.all_to_all(fresh, "x", 0, 0, tiled=True)
    fresh_copy = fresh.swapaxes(0, 1).reshape(rows, 2, kvw)
    return (new_master, new_momentum, fresh_copy)


def solution(mesh):
    split = Mesh(mesh.devices.reshape(2, 2, 8, 4, 4), ("yh", "core", "z", "yl", "x"))
    tensor, replica = ("yh", "core"), ("yl", "x")
    return jax.shard_map(
        body,
        mesh=split,
        in_specs=(
            P(replica, "z", tensor),
            P(replica, "z", None, tensor),
            P(replica, tensor + ("z",), None, None),
            P(replica, None),
            P(tensor + ("z",) + replica, None, None),
            P(tensor + ("z",) + replica, None, None),
        ),
        out_specs=(
            P(tensor + ("z",) + replica, None, None),
            P(tensor + ("z",) + replica, None, None),
            P(tensor + ("z",), None, None),
        ),
        check_vma=False,
    )
```

```python
import functools

import jax
import jax.numpy as jnp
from jax import lax
from jax.experimental import pallas as pl
from jax.experimental.pallas import tpu as pltpu
from jax.sharding import Mesh, PartitionSpec as P

inner_rate = 0.8
momentum_decay = 0.9
outer_rate = 0.7

f32, f16, bf16 = jnp.float32, jnp.float16, jnp.bfloat16


def product_kernel(n, place, acts, *rest):
    blocks, out = rest[:n], rest[n]
    part = blocks[0].shape[0] // 2
    first, second = (pl.ds(pl.multiple_of(place[n + i], 32), part) for i in range(2))
    tokens, values = [], []
    for i, block in enumerate(blocks):
        tokens.append(acts[place[i], first, :])
        values.append(block[...] if i > 0 else block[:part])
        if 0 < i < n - 1:
            tokens.append(acts[place[i], second, :])
    out[...] = lax.dot_general(
        jnp.concatenate(tokens, axis=0), jnp.concatenate(values, axis=0), (((0,), (0,)), ((), ())), preferred_element_type=f32
    )


def product(place, acts, blocks):
    rows, columns = acts.shape[2], blocks[0].shape[1]
    depth = acts.shape[0] * acts.shape[1] // 2
    return pl.pallas_call(
        functools.partial(product_kernel, len(blocks)),
        out_shape=jax.ShapeDtypeStruct((rows, columns), f32),
        in_specs=[pl.BlockSpec(memory_space=pltpu.SMEM)] + [pl.BlockSpec(memory_space=pltpu.VMEM)] * (1 + len(blocks)),
        out_specs=pl.BlockSpec(memory_space=pltpu.VMEM),
        compiler_params=pltpu.CompilerParams(vmem_limit_bytes=24 * 2**20),
        cost_estimate=pl.CostEstimate(
            flops=2 * depth * rows * columns, bytes_accessed=2 * depth * (rows + columns) + 4 * rows * columns, transcendentals=0
        ),
        name="token_half_product",
    )(place, acts, *blocks)


def body(activations, cotangents, inner_drift, drift_flags, master_weights, outer_momentum):
    n_z, replicas = lax.axis_size("z"), lax.axis_size("yl") * lax.axis_size("x")
    first_core = lax.axis_index("core") == 0
    low_half = lax.axis_index("yh") == 0
    z = lax.axis_index("z")
    tokens = activations.shape[1]
    part = tokens // 2
    own_rows = master_weights.shape[0]
    rows, kvw = inner_drift.shape[1], inner_drift.shape[3]
    half = kvw // 2

    def swap(value, axis):
        return lax.ppermute(value, axis, [(0, 1), (1, 0)])

    ways = [(i, (i + 1) % n_z) for i in range(n_z)] + [(n_z + i, n_z + (i - 1) % n_z) for i in range(n_z)]

    def step(value):
        return lax.ppermute(value, ("core", "z"), ways)

    def tied(*values):
        return lax.optimization_barrier(values)

    def chip(mine, other):
        mine, other = ([jnp.where(first_core, v, jnp.roll(v, part, axis=0)) for v in (w[0], w[1])] for w in (mine, other))
        pairs = [jnp.where(first_core, a, b) for k in range(2) for a, b in ((mine[k], other[k]), (other[k], mine[k]))]
        return jnp.concatenate(pairs, axis=1)

    def ring(block):
        held = [block]
        for _ in range(n_z // 2 - 1):
            block = step(block)
            held.append(block)
        held.append(step(block[:part]))
        return held

    acts = activations[0].reshape(tokens, n_z, rows).swapaxes(0, 1)
    acts = lax.all_to_all(acts, "z", 0, 0, tiled=True)
    acts_other = swap(acts, "core")
    sign = jnp.where(first_core, -1, 1)
    places = [(z + n_z + sign * s) % n_z for s in range(n_z // 2 + 1)]
    place = jnp.stack(places + [jnp.where(first_core, 0, part), jnp.where(first_core, part, 0)]).astype(jnp.int32)

    cots = cotangents[0].swapaxes(0, 1)
    far = swap(cots, "yh")
    near_held = ring(chip(cots, swap(cots, "core")))
    far_held = ring(chip(far, swap(far, "core")))

    flags = jnp.repeat(drift_flags[0].astype(f32), half)[None]
    drift = inner_drift[0].swapaxes(0, 1)

    def half_of(low):
        return jnp.concatenate(list(jnp.where(low, drift[:, :, :half], drift[:, :, half:])), axis=1)

    near_drift, far_drift, acts_other = tied(half_of(low_half), half_of(~low_half), acts_other)

    def term(held, drifts):
        came = swap(product(place, acts_other, held), "core")
        grads = product(place, acts, held) + came
        return (flags * (drifts + inner_rate * grads)).astype(f16)

    def reduced(value):
        got = lax.all_to_all(value.reshape(replicas, own_rows, -1), ("yl", "x"), 0, 0, tiled=True)
        return got.astype(f32).sum(0)

    near_term = term(near_held, near_drift)
    total = reduced(jnp.concatenate([near_term, term(far_held, far_drift)], axis=1))
    total = total.reshape(own_rows, 2, 2, half)
    low, high = jnp.where(low_half, total[:, 0], total[:, 1]), jnp.where(low_half, total[:, 1], total[:, 0])
    drift_sum = jnp.concatenate([low, high], axis=2)

    delta = drift_sum / replicas
    new_momentum = momentum_decay * outer_momentum + delta
    new_master = master_weights - outer_rate * (delta + momentum_decay * new_momentum)

    n_yl, n_x = lax.axis_size("yl"), lax.axis_size("x")
    fresh = jnp.broadcast_to(new_master.astype(bf16)[None], (n_yl, own_rows, 2, kvw))
    fresh = lax.all_to_all(fresh, "yl", 0, 0, tiled=True)
    fresh = jnp.broadcast_to(fresh[None], (n_x, n_yl, own_rows, 2, kvw))
    fresh = lax.all_to_all(fresh, "x", 0, 0, tiled=True)
    fresh_copy = fresh.swapaxes(0, 1).reshape(rows, 2, kvw)
    return (new_master, new_momentum, fresh_copy)


def solution(mesh):
    split = Mesh(mesh.devices.reshape(2, 2, 8, 4, 4), ("yh", "core", "z", "yl", "x"))
    tensor, replica = ("yh", "core"), ("yl", "x")
    return jax.shard_map(
        body,
        mesh=split,
        in_specs=(
            P(replica, "z", tensor),
            P(replica, "z", None, tensor),
            P(replica, tensor + ("z",), None, None),
            P(replica, None),
            P(tensor + ("z",) + replica, None, None),
            P(tensor + ("z",) + replica, None, None),
        ),
        out_specs=(
            P(tensor + ("z",) + replica, None, None),
            P(tensor + ("z",) + replica, None, None),
            P(tensor + ("z",), None, None),
        ),
        check_vma=False,
    )
```
